32 devices in a mesh: rep: 2 (over x), fsdp: 8 (over z, y), tp: 2 (over core).
Axes of the slice: x: 2, y: 2, z: 4, core: 2. Of those that a mesh axis runs over, the one named last changes fastest.
Arguments:
- states: bfloat16 [4, 32, 5120], P(None, 'rep', 'fsdp'), parts along dimension 1, may hold values from -24 to 24
- lengths: int32 [32], P(('rep', 'fsdp')), parts along dimension 0, may hold values from 1 to 512, as said below
- norm_gain: bfloat16 [5120], P('fsdp'), may hold values from 0.099609375 to 1.8984375
- query_weight: bfloat16 [5120, 8192], P('fsdp', 'tp'), may hold values from -0.078125 to 0.078125
- key_weight: bfloat16 [5120, 1024], P('fsdp', 'tp'), may hold values from -0.078125 to 0.078125
- value_weight: bfloat16 [5120, 1024], P('fsdp', 'tp'), may hold values from -0.078125 to 0.078125
- out_weight: bfloat16 [8192, 5120], P('tp', 'fsdp'), may hold values from -0.0625 to 0.0625
- query_down: bfloat16 [5120, 128], P('fsdp'), may hold values from -0.078125 to 0.078125
- query_up: bfloat16 [128, 8192], P('fsdp', 'tp'), may hold values from -0.5 to 0.5
- key_down: bfloat16 [5120, 128], P('fsdp'), may hold values from -0.078125 to 0.078125
- key_up: bfloat16 [128, 1024], P('fsdp', 'tp'), may hold values from -0.5 to 0.5
- value_down: bfloat16 [5120, 128], P('fsdp'), may hold values from -0.078125 to 0.078125
- value_up: bfloat16 [128, 1024], P('fsdp', 'tp'), may hold values from -0.5 to 0.5
- out_down: bfloat16 [8192, 128], P('tp', 'fsdp'), may hold values from -0.0625 to 0.0625
- out_up: bfloat16 [128, 5120], P(None, 'fsdp'), may hold values from -0.5 to 0.5
- key_cache: bfloat16 [32, 8, 512, 128], P(('rep', 'fsdp'), 'tp'), parts along dimension 0, may hold values from -260 to 260
- value_cache: bfloat16 [32, 8, 512, 128], P(('rep', 'fsdp'), 'tp'), parts along dimension 0, may hold values from -6 to 6
Outputs:
- next_states: bfloat16 [4, 32, 5120], P(None, 'rep', 'fsdp'), parts along dimension 1
The draws below stay inside these ranges and needn't reach their ends.
There are 2 independent parts, one for each index of `rep`. The reference program is written for one: setup_inputs(seed, part) draws one part's arguments, and reference() takes and returns one part's arrays. A program takes and returns all parts, laid end to end along the dimension named above; an argument that names none is the same for every part. Nothing has to cross between parts.
Inputs may be any that keep to these rules, and one draw needn't show every extreme that they name: `lengths`: every value from 1 to 512 may occur, and both ends occur in every draw.
All inputs are finite; a program needn't handle non-finite values.
Results may differ from the reference program's by a relative error of at most 0.0078.
Values may be sent and summed in bfloat16 or wider, within the bound.
A program may use at most 64 MiB of HBM per device.

```python
import jax
import jax.numpy as jnp
from jax import lax

D = 5120
HQ = 64
KVH = 8
HD = 128
R = 128
CACHE = 512
STEPS = 4
ROWS = 16


def draw_states(key, part):
    key = jax.random.fold_in(key, 11)
    first, second = jax.random.split(key, 2)
    ramp = 0.6 + 1.2 * jnp.arange(D, dtype=jnp.float32) / D
    logs = jax.random.uniform(second, (STEPS, ROWS, 1), jnp.float32, jnp.log(0.3), jnp.log(3.0))
    row_scale = jnp.exp(logs)
    base = jnp.clip(jax.random.normal(first, (STEPS, ROWS, D), jnp.float32), -4.0, 4.0)
    return (base * row_scale * ramp).astype(jnp.bfloat16)


def draw_lengths(key, part):
    key = jax.random.fold_in(key, 12)
    first, second = jax.random.split(key, 2)
    counts = jax.random.randint(first, (ROWS,), 1, CACHE + 1, dtype=jnp.int32)
    longest = jax.random.randint(second, (), 0, ROWS, dtype=jnp.int32)
    shortest = (longest + ROWS // 2) % ROWS
    index = jnp.arange(ROWS, dtype=jnp.int32)
    counts = jnp.where(index == longest, CACHE, counts)
    counts = jnp.where(index == shortest, 1, counts)
    return counts.astype(jnp.int32)


def draw_key_cache(key, part):
    key = jax.random.fold_in(key, 13)
    first = jax.random.fold_in(key, 0)
    base = jnp.clip(jax.random.normal(first, (ROWS, KVH, CACHE, HD), jnp.float32), -4.0, 4.0)
    return base.astype(jnp.bfloat16)


def block_scale(rng, shape, shards, smallest, top_value):
    level = 1.0
    for dim, parts in shards:
        draws = jax.random.uniform(jax.random.fold_in(jax.random.fold_in(rng, 6), dim), (parts,), jnp.float32, smallest / len(shards), top_value / len(shards))
        level = level * jnp.repeat(jnp.exp(draws), shape[dim] // parts).reshape((-1,) + (1,) * (len(shape) - 1 - dim))
    return level


def gaussian(own_key, dims, deviation, limit, pieces=(), kind=jnp.bfloat16):
    entries = jax.random.normal(own_key, dims, jnp.float32) * deviation
    if len(pieces) > 0:
        entries = block_scale(own_key, dims, pieces, -0.22, 0.18) * entries
    return jnp.clip(entries, min=-limit, max=limit).astype(kind)


def setup_inputs(seed: int = 0, part: int = 0) -> dict:
    splits = jax.random.split(jax.random.key(seed), 18)
    part_splits = jax.random.split(jax.random.fold_in(splits[17], part), 18)
    states = draw_states(jax.random.fold_in(jax.random.fold_in(splits[17], part), 71), part)
    lengths = draw_lengths(jax.random.fold_in(jax.random.fold_in(splits[17], part), 71), part)
    norm_gain = jnp.clip(1.0 + 0.18 * jax.random.normal(splits[2], (D,), jnp.float32), 0.099609375, 1.8984375).astype(jnp.bfloat16)
    query_weight = gaussian(splits[3], (D, HQ * HD), D ** -0.5, 0.078125, ((0, 8), (1, 2)))
    key_weight = gaussian(splits[4], (D, KVH * HD), D ** -0.5, 0.078125, ((0, 8), (1, 2)))
    value_weight = gaussian(splits[5], (D, KVH * HD), D ** -0.5, 0.078125, ((0, 8), (1, 2)))
    out_weight = gaussian(splits[6], (HQ * HD, D), (HQ * HD) ** -0.5, 0.0625, ((0, 2), (1, 8)))
    query_down = gaussian(splits[7], (D, R), D ** -0.5, 0.078125, ((0, 8),))
    query_up = gaussian(splits[8], (R, HQ * HD), R ** -0.5, 0.5, ((0, 8), (1, 2)))
    key_down = gaussian(splits[9], (D, R), D ** -0.5, 0.078125, ((0, 8),))
    key_up = gaussian(splits[10], (R, KVH * HD), R ** -0.5, 0.5, ((0, 8), (1, 2)))
    value_down = gaussian(splits[11], (D, R), D ** -0.5, 0.078125, ((0, 8),))
    value_up = gaussian(splits[12], (R, KVH * HD), R ** -0.5, 0.5, ((0, 8), (1, 2)))
    out_down = gaussian(splits[13], (HQ * HD, R), (HQ * HD) ** -0.5, 0.0625, ((0, 2), (1, 8)))
    out_up = gaussian(splits[14], (R, D), R ** -0.5, 0.5, ((1, 8),))
    key_cache = draw_key_cache(jax.random.fold_in(jax.random.fold_in(splits[17], part), 71), part)
    value_cache = gaussian(part_splits[16], (ROWS, KVH, CACHE, HD), 1.0, 6.0, ((0, 8), (1, 2)))
    return {"states": states, "lengths": lengths, "norm_gain": norm_gain, "query_weight": query_weight, "key_weight": key_weight, "value_weight": value_weight, "out_weight": out_weight, "query_down": query_down, "query_up": query_up, "key_down": key_down, "key_up": key_up, "value_down": value_down, "value_up": value_up, "out_down": out_down, "out_up": out_up, "key_cache": key_cache, "value_cache": value_cache}


EPS = 1e-06

def rotate(block, positions):
    count = block.shape[0]
    heads = block.shape[1] // HD
    half = HD // 2
    freq = jnp.power(jnp.float32(1000000.0), -(2.0 * jnp.arange(half, dtype=jnp.float32)) / HD)
    angle = positions.astype(jnp.float32)[:, None] * freq[None, :]
    cosine = jnp.cos(angle)[:, None, :]
    sine = jnp.sin(angle)[:, None, :]
    shaped = block.reshape(count, heads, HD)
    first = shaped[:, :, :half]
    second = shaped[:, :, half:]
    turned = jnp.concatenate([first * cosine - second * sine, second * cosine + first * sine], axis=2)
    return turned.reshape(count, heads * HD)

def split_heads(projected, query_cols, kv_cols, positions):
    count = projected.shape[0]
    kv_heads = kv_cols // HD
    group = query_cols // kv_cols
    queries = rotate(projected[:, :query_cols], positions).astype(jnp.bfloat16).reshape(count, kv_heads, group, HD)
    keys = rotate(projected[:, query_cols:query_cols + kv_cols], positions).astype(jnp.bfloat16).reshape(count, kv_heads, HD)
    values = projected[:, query_cols + kv_cols:].astype(jnp.bfloat16).reshape(count, kv_heads, HD)
    return (queries, keys, values)

def attend(queries, key_cache, value_cache, fresh_keys, fresh_values, lengths, step):
    count = queries.shape[0]
    factor = HD ** (-0.5)
    cached = jnp.einsum('rkgd,rkcd->rkgc', queries, key_cache, preferred_element_type=jnp.float32) * factor
    valid = jnp.arange(key_cache.shape[2], dtype=jnp.int32)[None, :] < lengths[:, None]
    cached = jnp.where(valid[:, None, None, :], cached, jnp.float32(-1e+30))
    fresh = jnp.einsum('rkgd,nrkd->rkgn', queries, fresh_keys, preferred_element_type=jnp.float32) * factor
    live = jnp.arange(fresh_keys.shape[0], dtype=jnp.int32) <= step
    fresh = jnp.where(live[None, None, None, :], fresh, jnp.float32(-1e+30))
    top = jnp.maximum(lax.optimization_barrier(jnp.max(cached, axis=-1)), lax.optimization_barrier(jnp.max(fresh, axis=-1)))
    cached_exp = jnp.exp(cached - top[..., None])
    fresh_exp = jnp.exp(fresh - top[..., None])
    total = lax.optimization_barrier(jnp.sum(cached_exp, axis=-1)) + lax.optimization_barrier(jnp.sum(fresh_exp, axis=-1))
    cached_w = (cached_exp / total[..., None]).astype(jnp.bfloat16)
    fresh_w = (fresh_exp / total[..., None]).astype(jnp.bfloat16)
    mixed = jnp.einsum('rkgc,rkcd->rkgd', cached_w, value_cache, preferred_element_type=jnp.float32)
    mixed = mixed + jnp.einsum('rkgn,nrkd->rkgd', fresh_w, fresh_values, preferred_element_type=jnp.float32)
    return mixed.astype(jnp.bfloat16).reshape(count, -1)

def reference(states, lengths, norm_gain, query_weight, key_weight, value_weight, out_weight, query_down, query_up, key_down, key_up, value_down, value_up, out_down, out_up, key_cache, value_cache):
    wide = states.astype(jnp.float32)
    meansq = lax.optimization_barrier(jnp.mean(wide * wide, axis=2))
    normed = (wide * lax.rsqrt(meansq + EPS)[..., None] * norm_gain.astype(jnp.float32)).astype(jnp.bfloat16)
    base = jnp.concatenate([query_weight, key_weight, value_weight], axis=1).astype(jnp.float32)
    delta = jnp.concatenate([jnp.dot(query_down, query_up, preferred_element_type=jnp.float32), jnp.dot(key_down, key_up, preferred_element_type=jnp.float32), jnp.dot(value_down, value_up, preferred_element_type=jnp.float32)], axis=1)
    qkv_merged = (base + delta).astype(jnp.bfloat16)
    out_merged = (out_weight.astype(jnp.float32) + jnp.dot(out_down, out_up, preferred_element_type=jnp.float32)).astype(jnp.bfloat16)
    query_cols = query_weight.shape[1]
    kv_cols = key_weight.shape[1]
    kept_keys = []
    kept_values = []
    results = []
    for step in range(STEPS):
        projected = jnp.dot(normed[step], qkv_merged, preferred_element_type=jnp.float32)
        queries, keys, values = split_heads(projected, query_cols, kv_cols, lengths + step)
        kept_keys.append(keys)
        kept_values.append(values)
        attended = attend(queries, key_cache, value_cache, jnp.stack(kept_keys), jnp.stack(kept_values), lengths, step)
        update = jnp.dot(attended, out_merged, preferred_element_type=jnp.float32)
        results.append((wide[step] + update).astype(jnp.bfloat16))
    return jnp.stack(results)
```

```python
import functools

import jax
import jax.numpy as jnp

import numpy as np
from jax import lax
from jax.experimental import pallas as pl
from jax.experimental.pallas import tpu as pltpu
from jax.sharding import PartitionSpec as P

D = 5120
HD = 128


EPS = 1e-06


def rotate(block, positions):
    count = block.shape[0]
    heads = block.shape[1] // HD
    half = HD // 2
    freq = jnp.power(jnp.float32(1000000.0), -(2.0 * jnp.arange(half, dtype=jnp.float32)) / HD)
    angle = positions.astype(jnp.float32)[:, None] * freq[None, :]
    cosine = jnp.cos(angle)[:, None, :]
    sine = jnp.sin(angle)[:, None, :]
    shaped = block.reshape(count, heads, HD)
    first = shaped[:, :, :half]
    second = shaped[:, :, half:]
    turned = jnp.concatenate(
        [first * cosine - second * sine, second * cosine + first * sine], axis=2
    )
    return turned.reshape(count, heads * HD)


def split_heads(projected, query_cols, kv_cols, positions):
    count = projected.shape[0]
    kv_heads = kv_cols // HD
    group = query_cols // kv_cols
    queries = (
        rotate(projected[:, :query_cols], positions)
        .astype(jnp.bfloat16)
        .reshape(count, kv_heads, group, HD)
    )
    keys = (
        rotate(projected[:, query_cols : query_cols + kv_cols], positions)
        .astype(jnp.bfloat16)
        .reshape(count, kv_heads, HD)
    )
    values = projected[:, query_cols + kv_cols :].astype(jnp.bfloat16).reshape(count, kv_heads, HD)
    return (queries, keys, values)


def attend(queries, key_cache, value_cache, fresh_keys, fresh_values, lengths, step):
    count = queries.shape[0]
    factor = HD ** (-0.5)
    cached = (
        jnp.einsum("rkgd,rkcd->rkgc", queries, key_cache, preferred_element_type=jnp.float32)
        * factor
    )
    valid = jnp.arange(key_cache.shape[2], dtype=jnp.int32)[None, :] < lengths[:, None]
    cached = jnp.where(valid[:, None, None, :], cached, jnp.float32(-1e30))
    fresh = (
        jnp.einsum("rkgd,nrkd->rkgn", queries, fresh_keys, preferred_element_type=jnp.float32)
        * factor
    )
    live = jnp.arange(fresh_keys.shape[0], dtype=jnp.int32) <= step
    fresh = jnp.where(live[None, None, None, :], fresh, jnp.float32(-1e30))
    top = jnp.maximum(jnp.max(cached, axis=-1), jnp.max(fresh, axis=-1))
    cached_exp = jnp.exp(cached - top[..., None])
    fresh_exp = jnp.exp(fresh - top[..., None])
    total = jnp.sum(cached_exp, axis=-1) + jnp.sum(fresh_exp, axis=-1)
    cached_w = (cached_exp / total[..., None]).astype(jnp.bfloat16)
    fresh_w = (fresh_exp / total[..., None]).astype(jnp.bfloat16)
    mixed = jnp.einsum("rkgc,rkcd->rkgd", cached_w, value_cache, preferred_element_type=jnp.float32)
    mixed = mixed + jnp.einsum(
        "rkgn,nrkd->rkgd", fresh_w, fresh_values, preferred_element_type=jnp.float32
    )
    return mixed.astype(jnp.bfloat16).reshape(count, -1)


def body(
    states,
    lengths,
    norm_gain,
    query_weight,
    key_weight,
    value_weight,
    out_weight,
    query_down,
    query_up,
    key_down,
    key_up,
    value_down,
    value_up,
    out_down,
    out_up,
    key_cache,
    value_cache,
):
    wide = states.astype(jnp.float32)
    squares = jnp.sum(wide * wide, axis=2)
    totals = lax.psum(squares, "fsdp")
    normed = (wide * lax.rsqrt(totals / D + EPS)[..., None] * norm_gain.astype(jnp.float32)).astype(
        jnp.bfloat16
    )
    query_full, key_full, value_full, out_full = (
        lax.all_gather(query_up, "fsdp", axis=0, tiled=True),
        lax.all_gather(key_up, "fsdp", axis=0, tiled=True),
        lax.all_gather(value_up, "fsdp", axis=0, tiled=True),
        lax.all_gather(out_down, "fsdp", axis=1, tiled=True),
    )
    base = jnp.concatenate([query_weight, key_weight, value_weight], axis=1).astype(jnp.float32)
    delta = jnp.concatenate(
        [
            jnp.dot(query_down, query_full, preferred_element_type=jnp.float32),
            jnp.dot(key_down, key_full, preferred_element_type=jnp.float32),
            jnp.dot(value_down, value_full, preferred_element_type=jnp.float32),
        ],
        axis=1,
    )
    qkv_merged = (base + delta).astype(jnp.bfloat16)
    out_merged = (
        out_weight.astype(jnp.float32)
        + jnp.dot(out_full, out_up, preferred_element_type=jnp.float32)
    ).astype(jnp.bfloat16)
    query_cols = query_weight.shape[1]
    kv_cols = key_weight.shape[1]
    step_count = states.shape[0]
    row_total = states.shape[1]
    row_count = row_total // lax.axis_size("fsdp")
    kept_keys = []
    kept_values = []
    results = []
    for step in range(step_count):
        slab = normed[step]

        def project(start, count, slab=slab):
            return jnp.dot(slab, qkv_merged, preferred_element_type=jnp.float32)

        projected = lax.psum_scatter(
            project(jnp.int32(0), row_count * lax.axis_size("fsdp")),
            "fsdp",
            scatter_dimension=0,
            tiled=True,
        )
        queries, keys, values = split_heads(projected, query_cols, kv_cols, lengths + step)
        kept_keys.append(keys)
        kept_values.append(values)
        attended = attend(
            queries,
            key_cache,
            value_cache,
            jnp.stack(kept_keys),
            jnp.stack(kept_values),
            lengths,
            step,
        )
        partial_value = jnp.dot(
            lax.all_gather(attended, "fsdp", axis=0, tiled=True),
            out_merged,
            preferred_element_type=jnp.float32,
        )
        summed = lax.psum(partial_value, "tp")
        results.append((wide[step] + summed).astype(jnp.bfloat16))
    return jnp.stack(results)


def fused_kernel(
    cfg,
    len_ref,
    x_hbm,
    gain_hbm,
    qd_hbm,
    kd_hbm,
    vd_hbm,
    qu_hbm,
    ku_hbm,
    vu_hbm,
    od_hbm,
    ou_hbm,
    perm_hbm,
    back_hbm,
    freq_hbm,
    qw_hbm,
    kw_hbm,
    vw_hbm,
    ow_hbm,
    kc_hbm,
    vc_hbm,
    out_ref,
    x_ref,
    gain_ref,
    qd_ref,
    kd_ref,
    vd_ref,
    qu_ref,
    ku_ref,
    vu_ref,
    od_ref,
    ou_ref,
    perm_ref,
    back_ref,
    freq_ref,
    w_buf,
    ow_buf,
    kc_buf,
    vc_buf,
    t_send,
    t_recv,
    p_send,
    p_recv,
    a_buf,
    u_buf,
    o_send,
    o_recv,
    s_sem,
    w_sem,
    ow_sem,
    c_sem,
    t_ssem,
    t_rsem,
    p_ssem,
    p_rsem,
    a_ssem,
    a_rsem,
    u_ssem,
    u_rsem,
    o_ssem,
    o_rsem,
):
    n, tp, steps, rc = cfg
    f32 = jnp.float32
    bf16 = jnp.bfloat16
    me = lax.axis_index("fsdp")
    mt = lax.axis_index("tp")
    rows = x_ref.shape[0]
    m = steps * rc
    chunk = kw_hbm.shape[1]
    qn = qw_hbm.shape[1] // chunk
    chunks = qn + 2
    groups = chunks // 2
    kv = chunk // HD
    group = qn
    rank = qu_ref.shape[0]

    def peer(d):
        return lax.rem(me + d, n)

    def remote(src, dst, ssem, rsem, d, e=0):
        return pltpu.make_async_remote_copy(
            src_ref=src,
            dst_ref=dst,
            send_sem=ssem,
            recv_sem=rsem,
            device_id={"fsdp": peer(d), "tp": lax.rem(mt + e, tp)},
            device_id_type=pl.DeviceIdType.MESH,
        )

    def weight_copy(c):
        if c < qn:
            src = qw_hbm.at[:, pl.ds(c * chunk, chunk)]
        elif c == qn:
            src = kw_hbm
        else:
            src = vw_hbm
        return pltpu.make_async_copy(src, w_buf.at[c], w_sem.at[c])

    small = [
        pltpu.make_async_copy(src, dst, s_sem.at[i])
        for i, (src, dst) in enumerate(
            (
                (perm_hbm, perm_ref),
                (x_hbm, x_ref),
                (gain_hbm, gain_ref),
                (qd_hbm, qd_ref),
                (kd_hbm, kd_ref),
                (vd_hbm, vd_ref),
                (qu_hbm, qu_ref),
                (ku_hbm, ku_ref),
                (vu_hbm, vu_ref),
                (freq_hbm, freq_ref),
                (back_hbm, back_ref),
                (od_hbm, od_ref),
                (ou_hbm, ou_ref),
            )
        )
    ]
    for copy in small:
        copy.start()
    order = []
    for g in range(groups):
        order += [g, groups + g]
    loads = {}
    for c in order:
        loads[c] = weight_copy(c)
        loads[c].start()
    kc_load = pltpu.make_async_copy(kc_hbm, kc_buf, c_sem.at[0])
    vc_load = pltpu.make_async_copy(vc_hbm, vc_buf, c_sem.at[1])
    ow_load = pltpu.make_async_copy(ow_hbm, ow_buf, ow_sem)
    kc_load.start()
    vc_load.start()
    ow_load.start()

    barrier = pltpu.get_barrier_semaphore()
    others = [(d, e) for e in range(tp) for d in range(n) if d or e]
    for d, e in others:
        pl.semaphore_signal(
            barrier,
            inc=1,
            device_id={"fsdp": peer(d), "tp": lax.rem(mt + e, tp)},
            device_id_type=pl.DeviceIdType.MESH,
        )

    for copy in small[:6]:
        copy.wait()
    xp = jnp.dot(perm_ref[...], x_ref[...], preferred_element_type=f32)
    square = jnp.sum(xp[:rows] * xp[:rows], axis=1, keepdims=True)
    xg = (xp * gain_ref[...].astype(f32)).astype(bf16)
    lanes = xg.shape[0]
    nt = (((0,), (1,)), ((), ()))
    tt = [
        lax.dot_general(ref[...], xg, nt, preferred_element_type=f32)
        for ref in (qd_ref, kd_ref, vd_ref)
    ]
    for p in range(n):
        for i in range(3):
            t_send[p, i * rank : (i + 1) * rank, :] = tt[i][p * rank : (p + 1) * rank, :]
        t_send[p, 3 * rank : 3 * rank + m, :] = jnp.broadcast_to(
            square[p * m : (p + 1) * m], (m, lanes)
        )
    pl.semaphore_wait(barrier, len(others))
    sends = []
    t_copies = []
    for d in range(1, n):
        copy = remote(t_send.at[peer(d)], t_recv.at[d - 1], t_ssem.at[d - 1], t_rsem.at[d - 1], d)
        copy.start()
        t_copies.append(copy)
        sends.append(copy)

    xm = xg[:rows]

    def base(c):
        loads[c].wait()
        return jnp.dot(xm, w_buf[c], preferred_element_type=f32)

    first = [base(0), base(groups)]
    for copy in small[6:9]:
        copy.wait()
    tsum = t_send[me]
    for d in range(1, n):
        t_copies[d - 1].wait_recv()
        tsum = tsum + t_recv[d - 1]
    low = [tsum[i * rank : (i + 1) * rank].astype(bf16) for i in range(3)]
    scale = lax.rsqrt(tsum[3 * rank : 3 * rank + m] / D + EPS)
    tn = (((0,), (0,)), ((), ()))

    def delta(c):
        if c < qn:
            up, left = qu_ref[:, c * chunk : (c + 1) * chunk], low[0]
        elif c == qn:
            up, left = ku_ref[...], low[1]
        else:
            up, left = vu_ref[...], low[2]
        return lax.dot_general(left, up, tn, preferred_element_type=f32)[:rows]

    p_copies = []
    for g in range(groups):
        if g == 0:
            lo, hi = first
        else:
            lo, hi = base(g), base(groups + g)
        lo = lo + delta(g)
        hi = hi + delta(groups + g)
        both = jnp.concatenate(
            [lo.reshape(n, m, chunk), hi.reshape(n, m, chunk)], axis=1
        )
        p_send[g] = both.astype(bf16)
        for d in range(1, n):
            copy = remote(
                p_send.at[g, peer(d)],
                p_recv.at[g, d - 1],
                p_ssem.at[g, d - 1],
                p_rsem.at[g, d - 1],
                d,
            )
            copy.start()
            p_copies.append(copy)
            sends.append(copy)

    for copy in small[9:]:
        copy.wait()
    index = lax.broadcasted_iota(jnp.int32, (m, HD), 0)
    row = lax.rem(index, jnp.int32(rc))
    position = lax.div(index, jnp.int32(rc))
    for r in range(rc):
        position = position + jnp.where(row == r, len_ref[r], 0)
    angle = position.astype(f32) * freq_ref[0:1, :]
    cosine = jnp.cos(angle)
    sine = jnp.sin(angle) * freq_ref[1:2, :]

    halves = [[], []]
    k_next = 0
    for g in range(groups):
        total = p_send[g, me].astype(f32)
        for d in range(1, n):
            p_copies[k_next].wait_recv()
            k_next += 1
            total = total + p_recv[g, d - 1].astype(f32)
        halves[0].append(total[:m])
        halves[1].append(total[m:])
    parts = halves[0] + halves[1]

    def head(c, j):
        return parts[c][:, j * HD : (j + 1) * HD] * scale[:, :HD]

    def turned(block):
        swapped = jnp.concatenate([block[:, HD // 2 :], block[:, : HD // 2]], axis=1)
        return block * cosine + swapped * sine

    kc_load.wait()
    vc_load.wait()
    factor = HD ** (-0.5)
    q_rows = group * m
    cache = kc_buf.shape[2]
    q_index = lax.rem(lax.broadcasted_iota(jnp.int32, (q_rows, 1), 0), jnp.int32(m))
    q_row = lax.rem(q_index, jnp.int32(rc))
    q_step = lax.div(q_index, jnp.int32(rc))
    limit = jnp.zeros((q_rows, 1), jnp.int32)
    for r in range(rc):
        limit = limit + jnp.where(q_row == r, len_ref[r], 0)
    column = lax.broadcasted_iota(jnp.int32, (q_rows, cache), 1)
    valid = column < limit
    pad = 16
    f_col = lax.broadcasted_iota(jnp.int32, (q_rows, pad), 1)
    fresh_ok = (
        (f_col < m)
        & (lax.rem(f_col, jnp.int32(rc)) == q_row)
        & (lax.div(f_col, jnp.int32(rc)) <= q_step)
    )
    nn = (((1,), (1,)), ((), ()))
    zeros = jnp.zeros((pad - m, HD), f32)
    heads = []
    for k in range(kv):
        tiles = []
        for j in range(group):
            h = k * group + j
            tiles.append(turned(head(h // kv, h % kv)))
        q = jnp.concatenate(tiles, axis=0).astype(bf16)
        new_k = jnp.concatenate([turned(head(qn, k)), zeros], axis=0).astype(bf16)
        new_v = jnp.concatenate([head(qn + 1, k), zeros], axis=0).astype(bf16)
        score = jnp.zeros((q_rows, cache), f32)
        for r in range(rc):
            one = lax.dot_general(q, kc_buf[r, k], nn, preferred_element_type=f32)
            score = jnp.where(q_row == r, one, score)
        score = jnp.where(valid, score * factor, -1e30)
        fresh = lax.dot_general(q, new_k, nn, preferred_element_type=f32) * factor
        fresh = jnp.where(fresh_ok, fresh, -1e30)
        top = jnp.maximum(
            jnp.max(score, axis=1, keepdims=True), jnp.max(fresh, axis=1, keepdims=True)
        )
        e_score = jnp.exp(score - top)
        e_fresh = jnp.exp(fresh - top)
        inverse = 1.0 / (
            jnp.sum(e_score, axis=1, keepdims=True) + jnp.sum(e_fresh, axis=1, keepdims=True)
        )
        weight = (e_score * inverse).astype(bf16)
        mixed = jnp.dot(
            (e_fresh * inverse).astype(bf16), new_v, preferred_element_type=f32
        )
        for r in range(rc):
            one = jnp.dot(weight, vc_buf[r, k], preferred_element_type=f32)
            mixed = mixed + jnp.where(q_row == r, one, 0.0)
        for j in range(group):
            heads.append(mixed[j * m : (j + 1) * m])
    half = len(heads) // 2
    both = jnp.concatenate(
        [jnp.concatenate(heads[:half], axis=1), jnp.concatenate(heads[half:], axis=1)], axis=0
    )
    a_buf[me] = both.astype(bf16)
    a_copies = []
    for d in range(1, n):
        copy = remote(a_buf.at[me], a_buf.at[me], a_ssem.at[d - 1], a_rsem.at[d - 1], d)
        copy.start()
        a_copies.append(copy)
        sends.append(copy)
    ow_load.wait()
    for copy in a_copies:
        copy.wait_recv()

    flat = a_buf[...].reshape(n * 2 * m, -1)
    lo = jnp.dot(back_ref[0], flat, preferred_element_type=f32).astype(bf16)
    hi = jnp.dot(back_ref[1], flat, preferred_element_type=f32).astype(bf16)
    split = lo.shape[1]
    u = lax.dot_general(od_ref[:, :split], lo, nn, preferred_element_type=f32)
    u = u + lax.dot_general(od_ref[:, split:], hi, nn, preferred_element_type=f32)
    u_buf[mt, me] = u
    u_copies = []
    for i, (d, e) in enumerate(others):
        copy = remote(
            u_buf.at[mt, me], u_buf.at[mt, me], u_ssem.at[i], u_rsem.at[i], d, e
        )
        copy.start()
        u_copies.append(copy)
        sends.append(copy)
    o_send[...] = jnp.dot(
        lo[:rows], ow_buf[:split, :], preferred_element_type=f32
    ) + jnp.dot(hi[:rows], ow_buf[split:, :], preferred_element_type=f32)
    if tp > 1:
        o_copy = remote(o_send, o_recv, o_ssem, o_rsem, 0, 1)
        o_copy.start()
        sends.append(o_copy)
    for copy in u_copies:
        copy.wait_recv()
    whole = u_buf[0]
    for t in range(1, tp):
        whole = whole + u_buf[t]
    whole = whole.reshape(n * rank, lanes).astype(bf16)
    result = lax.dot_general(whole, ou_ref[...], tn, preferred_element_type=f32)[:rows]
    result = result + x_ref[...].astype(f32)
    if tp > 1:
        o_copy.wait_recv()
        result = result + (o_send[...] + o_recv[...])
    else:
        result = result + o_send[...]
    out_ref[...] = result.astype(out_ref.dtype)
    for copy in sends:
        copy.wait_send()


def fused(n, tp, *args):
    (
        states,
        lengths,
        norm_gain,
        query_weight,
        key_weight,
        value_weight,
        out_weight,
        query_down,
        query_up,
        key_down,
        key_up,
        value_down,
        value_up,
        out_down,
        out_up,
        key_cache,
        value_cache,
    ) = args
    steps, row_total, width = states.shape
    rc = row_total // n
    rows = steps * row_total
    m = steps * rc
    rank = query_up.shape[0]
    chunk = key_weight.shape[1]
    chunks = query_weight.shape[1] // chunk + 2
    groups = chunks // 2
    lanes = -(-rows // 128) * 128
    bf16 = jnp.bfloat16
    f32 = jnp.float32

    perm = np.zeros((lanes, rows), np.float32)
    back = np.zeros((2, lanes, n * 2 * m), np.float32)
    for p in range(n):
        for s in range(steps):
            for r in range(rc):
                natural = s * row_total + p * rc + r
                perm[p * m + s * rc + r, natural] = 1
                for side in range(2):
                    back[side, natural, p * 2 * m + side * m + s * rc + r] = 1
    half = HD // 2
    freq = np.power(1000000.0, -(2.0 * np.arange(half)) / HD)
    table = np.zeros((8, HD), np.float32)
    table[0] = np.concatenate([freq, freq])
    table[1] = np.concatenate([-np.ones(half), np.ones(half)])

    vmem = pl.BlockSpec(memory_space=pltpu.VMEM)
    smem = pl.BlockSpec(memory_space=pltpu.SMEM)
    hbm = pl.BlockSpec(memory_space=pl.ANY)
    dma = pltpu.SemaphoreType.DMA
    att = query_weight.shape[1] // 2
    out = pl.pallas_call(
        functools.partial(fused_kernel, (n, tp, steps, rc)),
        out_shape=jax.ShapeDtypeStruct((rows, width), states.dtype),
        in_specs=[smem] + [hbm] * 19,
        out_specs=vmem,
        scratch_shapes=[
            pltpu.VMEM((rows, width), bf16),
            pltpu.VMEM((1, width), bf16),
            pltpu.VMEM(query_down.shape, bf16),
            pltpu.VMEM(key_down.shape, bf16),
            pltpu.VMEM(value_down.shape, bf16),
            pltpu.VMEM(query_up.shape, bf16),
            pltpu.VMEM(key_up.shape, bf16),
            pltpu.VMEM(value_up.shape, bf16),
            pltpu.VMEM(out_down.shape[::-1], bf16),
            pltpu.VMEM(out_up.shape, bf16),
            pltpu.VMEM(perm.shape, bf16),
            pltpu.VMEM(back.shape, bf16),
            pltpu.VMEM(table.shape, f32),
            pltpu.VMEM((chunks, width, chunk), bf16),
            pltpu.VMEM(out_weight.shape, bf16),
            pltpu.VMEM(key_cache.shape, bf16),
            pltpu.VMEM(value_cache.shape, bf16),
            pltpu.VMEM((n, 3 * rank + m, lanes), f32),
            pltpu.VMEM((n - 1, 3 * rank + m, lanes), f32),
            pltpu.VMEM((groups, n, 2 * m, chunk), bf16),
            pltpu.VMEM((groups, n - 1, 2 * m, chunk), bf16),
            pltpu.VMEM((n, 2 * m, att), bf16),
            pltpu.VMEM((tp, n, rank, lanes), f32),
            pltpu.VMEM((rows, width), f32),
            pltpu.VMEM((rows, width), f32),
            dma((13,)),
            dma((chunks,)),
            dma,
            dma((2,)),
            dma((n - 1,)),
            dma((n - 1,)),
            dma((groups, n - 1)),
            dma((groups, n - 1)),
            dma((n - 1,)),
            dma((n - 1,)),
            dma((n * tp - 1,)),
            dma((n * tp - 1,)),
            dma,
            dma,
        ],
        compiler_params=pltpu.CompilerParams(
            collective_id=0, has_side_effects=True, vmem_limit_bytes=56 * 2**20
        ),
    )(
        lengths,
        states.reshape(rows, width),
        norm_gain.reshape(1, width),
        query_down,
        key_down,
        value_down,
        query_up,
        key_up,
        value_up,
        out_down.T,
        out_up,
        jnp.asarray(perm, bf16),
        jnp.asarray(back, bf16),
        jnp.asarray(table),
        query_weight,
        key_weight,
        value_weight,
        out_weight,
        key_cache,
        value_cache,
    )
    return out.reshape(states.shape)


def fits(n, tp, states, lengths, query_weight, key_weight, query_up):
    m = states.shape[0] * lengths.shape[0]
    return (
        n > 1
        and n <= 8
        and tp == 2
        and m == 8
        and states.shape[2] % 128 == 0
        and query_up.shape[0] % 16 == 0
        and query_weight.shape[1] % (2 * key_weight.shape[1]) == 0
    )


def choose(n, tp, *args):
    if fits(n, tp, args[0], args[1], args[3], args[4], args[8]):
        return fused(n, tp, *args)
    return body(*args)


def solution(mesh):
    in_specs = (
        P(None, "rep", "fsdp"),
        P(("rep", "fsdp")),
        P("fsdp"),
        P("fsdp", "tp"),
        P("fsdp", "tp"),
        P("fsdp", "tp"),
        P("tp", "fsdp"),
        P("fsdp", None),
        P("fsdp", "tp"),
        P("fsdp", None),
        P("fsdp", "tp"),
        P("fsdp", None),
        P("fsdp", "tp"),
        P("tp", "fsdp"),
        P(None, "fsdp"),
        P(("rep", "fsdp"), "tp", None, None),
        P(("rep", "fsdp"), "tp", None, None),
    )
    out_specs = P(None, "rep", "fsdp")
    return jax.shard_map(functools.partial(choose, mesh.shape["fsdp"], mesh.shape["tp"]), mesh=mesh, in_specs=in_specs, out_specs=out_specs, check_vma=False)
```

```python
import functools

import jax
import jax.numpy as jnp

import numpy as np
from jax import lax
from jax.experimental import pallas as pl
from jax.experimental.pallas import tpu as pltpu
from jax.sharding import PartitionSpec as P

D = 5120
HD = 128


EPS = 1e-06


def rotate(block, positions):
    count = block.shape[0]
    heads = block.shape[1] // HD
    half = HD // 2
    freq = jnp.power(jnp.float32(1000000.0), -(2.0 * jnp.arange(half, dtype=jnp.float32)) / HD)
    angle = positions.astype(jnp.float32)[:, None] * freq[None, :]
    cosine = jnp.cos(angle)[:, None, :]
    sine = jnp.sin(angle)[:, None, :]
    shaped = block.reshape(count, heads, HD)
    first = shaped[:, :, :half]
    second = shaped[:, :, half:]
    turned = jnp.concatenate(
        [first * cosine - second * sine, second * cosine + first * sine], axis=2
    )
    return turned.reshape(count, heads * HD)


def split_heads(projected, query_cols, kv_cols, positions):
    count = projected.shape[0]
    kv_heads = kv_cols // HD
    group = query_cols // kv_cols
    queries = (
        rotate(projected[:, :query_cols], positions)
        .astype(jnp.bfloat16)
        .reshape(count, kv_heads, group, HD)
    )
    keys = (
        rotate(projected[:, query_cols : query_cols + kv_cols], positions)
        .astype(jnp.bfloat16)
        .reshape(count, kv_heads, HD)
    )
    values = projected[:, query_cols + kv_cols :].astype(jnp.bfloat16).reshape(count, kv_heads, HD)
    return (queries, keys, values)


def attend(queries, key_cache, value_cache, fresh_keys, fresh_values, lengths, step):
    count = queries.shape[0]
    factor = HD ** (-0.5)
    cached = (
        jnp.einsum("rkgd,rkcd->rkgc", queries, key_cache, preferred_element_type=jnp.float32)
        * factor
    )
    valid = jnp.arange(key_cache.shape[2], dtype=jnp.int32)[None, :] < lengths[:, None]
    cached = jnp.where(valid[:, None, None, :], cached, jnp.float32(-1e30))
    fresh = (
        jnp.einsum("rkgd,nrkd->rkgn", queries, fresh_keys, preferred_element_type=jnp.float32)
        * factor
    )
    live = jnp.arange(fresh_keys.shape[0], dtype=jnp.int32) <= step
    fresh = jnp.where(live[None, None, None, :], fresh, jnp.float32(-1e30))
    top = jnp.maximum(jnp.max(cached, axis=-1), jnp.max(fresh, axis=-1))
    cached_exp = jnp.exp(cached - top[..., None])
    fresh_exp = jnp.exp(fresh - top[..., None])
    total = jnp.sum(cached_exp, axis=-1) + jnp.sum(fresh_exp, axis=-1)
    cached_w = (cached_exp / total[..., None]).astype(jnp.bfloat16)
    fresh_w = (fresh_exp / total[..., None]).astype(jnp.bfloat16)
    mixed = jnp.einsum("rkgc,rkcd->rkgd", cached_w, value_cache, preferred_element_type=jnp.float32)
    mixed = mixed + jnp.einsum(
        "rkgn,nrkd->rkgd", fresh_w, fresh_values, preferred_element_type=jnp.float32
    )
    return mixed.astype(jnp.bfloat16).reshape(count, -1)


def body(
    states,
    lengths,
    norm_gain,
    query_weight,
    key_weight,
    value_weight,
    out_weight,
    query_down,
    query_up,
    key_down,
    key_up,
    value_down,
    value_up,
    out_down,
    out_up,
    key_cache,
    value_cache,
):
    wide = states.astype(jnp.float32)
    squares = jnp.sum(wide * wide, axis=2)
    totals = lax.psum(squares, "fsdp")
    normed = (wide * lax.rsqrt(totals / D + EPS)[..., None] * norm_gain.astype(jnp.float32)).astype(
        jnp.bfloat16
    )
    query_full, key_full, value_full, out_full = (
        lax.all_gather(query_up, "fsdp", axis=0, tiled=True),
        lax.all_gather(key_up, "fsdp", axis=0, tiled=True),
        lax.all_gather(value_up, "fsdp", axis=0, tiled=True),
        lax.all_gather(out_down, "fsdp", axis=1, tiled=True),
    )
    base = jnp.concatenate([query_weight, key_weight, value_weight], axis=1).astype(jnp.float32)
    delta = jnp.concatenate(
        [
            jnp.dot(query_down, query_full, preferred_element_type=jnp.float32),
            jnp.dot(key_down, key_full, preferred_element_type=jnp.float32),
            jnp.dot(value_down, value_full, preferred_element_type=jnp.float32),
        ],
        axis=1,
    )
    qkv_merged = (base + delta).astype(jnp.bfloat16)
    out_merged = (
        out_weight.astype(jnp.float32)
        + jnp.dot(out_full, out_up, preferred_element_type=jnp.float32)
    ).astype(jnp.bfloat16)
    query_cols = query_weight.shape[1]
    kv_cols = key_weight.shape[1]
    step_count = states.shape[0]
    row_total = states.shape[1]
    row_count = row_total // lax.axis_size("fsdp")
    kept_keys = []
    kept_values = []
    results = []
    for step in range(step_count):
        slab = normed[step]

        def project(start, count, slab=slab):
            return jnp.dot(slab, qkv_merged, preferred_element_type=jnp.float32)

        projected = lax.psum_scatter(
            project(jnp.int32(0), row_count * lax.axis_size("fsdp")),
            "fsdp",
            scatter_dimension=0,
            tiled=True,
        )
        queries, keys, values = split_heads(projected, query_cols, kv_cols, lengths + step)
        kept_keys.append(keys)
        kept_values.append(values)
        attended = attend(
            queries,
            key_cache,
            value_cache,
            jnp.stack(kept_keys),
            jnp.stack(kept_values),
            lengths,
            step,
        )
        partial_value = jnp.dot(
            lax.all_gather(attended, "fsdp", axis=0, tiled=True),
            out_merged,
            preferred_element_type=jnp.float32,
        )
        summed = lax.psum(partial_value, "tp")
        results.append((wide[step] + summed).astype(jnp.bfloat16))
    return jnp.stack(results)


def fused_kernel(
    cfg,
    len_ref,
    x_hbm,
    gain_hbm,
    qd_hbm,
    kd_hbm,
    vd_hbm,
    qu_hbm,
    ku_hbm,
    vu_hbm,
    od_hbm,
    ou_hbm,
    perm_hbm,
    back_hbm,
    freq_hbm,
    qw_hbm,
    kw_hbm,
    vw_hbm,
    ow_hbm,
    kc_hbm,
    vc_hbm,
    out_ref,
    x_ref,
    gain_ref,
    qd_ref,
    kd_ref,
    vd_ref,
    qu_ref,
    ku_ref,
    vu_ref,
    od_ref,
    ou_ref,
    perm_ref,
    back_ref,
    freq_ref,
    w_buf,
    ow_buf,
    kc_buf,
    vc_buf,
    t_send,
    t_recv,
    p_send,
    y_recv,
    mid,
    p_recv,
    a_buf,
    u_buf,
    o_send,
    o_recv,
    s_sem,
    w_sem,
    ow_sem,
    c_sem,
    t_ssem,
    t_rsem,
    y_ssem,
    y_rsem,
    p_ssem,
    p_rsem,
    a_ssem,
    a_rsem,
    u_ssem,
    u_rsem,
    o_ssem,
    o_rsem,
):
    n, tp, steps, rc = cfg
    f32 = jnp.float32
    bf16 = jnp.bfloat16
    me = lax.axis_index("fsdp")
    mt = lax.axis_index("tp")
    rows = x_ref.shape[0]
    m = steps * rc
    chunk = kw_hbm.shape[1]
    qn = qw_hbm.shape[1] // chunk
    chunks = qn + 2
    groups = chunks // 2
    kv = chunk // HD
    group = qn
    rank = qu_ref.shape[0]

    def peer(d):
        return lax.rem(me + d, n)

    def remote(src, dst, ssem, rsem, d, e=0):
        return pltpu.make_async_remote_copy(
            src_ref=src,
            dst_ref=dst,
            send_sem=ssem,
            recv_sem=rsem,
            device_id={"fsdp": peer(d), "tp": lax.rem(mt + e, tp)},
            device_id_type=pl.DeviceIdType.MESH,
        )

    side_of = lax.rem(me, 2)
    place = lax.div(me, 2)
    far = n // 2
    partner = me + 1 - 2 * side_of

    def remote_to(src, dst, ssem, rsem, device):
        return pltpu.make_async_remote_copy(
            src_ref=src,
            dst_ref=dst,
            send_sem=ssem,
            recv_sem=rsem,
            device_id={"fsdp": device, "tp": mt},
            device_id_type=pl.DeviceIdType.MESH,
        )

    def weight_copy(c):
        if c < qn:
            src = qw_hbm.at[:, pl.ds(c * chunk, chunk)]
        elif c == qn:
            src = kw_hbm
        else:
            src = vw_hbm
        return pltpu.make_async_copy(src, w_buf.at[c], w_sem.at[c])

    small = [
        pltpu.make_async_copy(src, dst, s_sem.at[i])
        for i, (src, dst) in enumerate(
            (
                (perm_hbm, perm_ref),
                (x_hbm, x_ref),
                (gain_hbm, gain_ref),
                (qd_hbm, qd_ref),
                (kd_hbm, kd_ref),
                (vd_hbm, vd_ref),
                (qu_hbm, qu_ref),
                (ku_hbm, ku_ref),
                (vu_hbm, vu_ref),
                (freq_hbm, freq_ref),
                (back_hbm, back_ref),
                (od_hbm, od_ref),
                (ou_hbm, ou_ref),
            )
        )
    ]
    for copy in small:
        copy.start()
    pairs = [(qn, qn + 1)] + [(c, c + qn // 2) for c in range(qn // 2)]
    order = [c for pair in pairs for c in pair]
    loads = {}
    for c in order:
        loads[c] = weight_copy(c)
        loads[c].start()
    kc_load = pltpu.make_async_copy(kc_hbm, kc_buf, c_sem.at[0])
    vc_load = pltpu.make_async_copy(vc_hbm, vc_buf, c_sem.at[1])
    ow_load = pltpu.make_async_copy(ow_hbm, ow_buf, ow_sem)
    kc_load.start()
    vc_load.start()
    ow_load.start()

    barrier = pltpu.get_barrier_semaphore()
    others = [(d, e) for e in range(tp) for d in range(n) if d or e]
    for d, e in others:
        pl.semaphore_signal(
            barrier,
            inc=1,
            device_id={"fsdp": peer(d), "tp": lax.rem(mt + e, tp)},
            device_id_type=pl.DeviceIdType.MESH,
        )

    for copy in small[:6]:
        copy.wait()
    xp = jnp.dot(perm_ref[...], x_ref[...], preferred_element_type=f32)
    square = jnp.sum(xp[:rows] * xp[:rows], axis=1, keepdims=True)
    xg = (xp * gain_ref[...].astype(f32).reshape(1, -1)).astype(bf16)
    lanes = xg.shape[0]
    nt = (((0,), (1,)), ((), ()))
    tt = [
        lax.dot_general(ref[...], xg, nt, preferred_element_type=f32)
        for ref in (qd_ref, kd_ref, vd_ref)
    ]
    for p in range(n):
        for i in range(3):
            t_send[p, i * rank : (i + 1) * rank, :] = tt[i][p * rank : (p + 1) * rank, :]
        t_send[p, 3 * rank : 3 * rank + m, :] = jnp.broadcast_to(
            square[(p % 2 * far + p // 2) * m : (p % 2 * far + p // 2 + 1) * m], (m, lanes)
        )
    pl.semaphore_wait(barrier, len(others))
    sends = []
    t_copies = []
    for d in range(1, n):
        copy = remote(t_send.at[peer(d)], t_recv.at[d - 1], t_ssem.at[d - 1], t_rsem.at[d - 1], d)
        copy.start()
        t_copies.append(copy)
        sends.append(copy)

    xm = xg[:rows]

    def base(c):
        loads[c].wait()
        return jnp.dot(xm, w_buf[c], preferred_element_type=f32)

    first = [base(c) for c in pairs[0]]
    for copy in small[6:9]:
        copy.wait()
    tsum = t_send[me]
    for d in range(1, n):
        t_copies[d - 1].wait_recv()
        tsum = tsum + t_recv[d - 1]
    low = [tsum[i * rank : (i + 1) * rank].astype(bf16) for i in range(3)]
    scale = lax.rsqrt(tsum[3 * rank : 3 * rank + m] / D + EPS)
    tn = (((0,), (0,)), ((), ()))

    def delta(c):
        if c < qn:
            up, left = qu_ref[:, c * chunk : (c + 1) * chunk], low[0]
        elif c == qn:
            up, left = ku_ref[...], low[1]
        else:
            up, left = vu_ref[...], low[2]
        return lax.dot_general(left, up, tn, preferred_element_type=f32)[:rows]

    p_copies = []
    y_copies = []

    def spread(g):
        y_copies[g].wait_recv()
        joined = p_send[g, side_of].astype(f32) + y_recv[g].astype(f32)
        mid[g] = joined.astype(bf16)
        for d in range(1, far):
            z = lax.rem(place + d, far)
            copy = remote_to(
                mid.at[g, z],
                p_recv.at[g, d - 1],
                p_ssem.at[g, d - 1],
                p_rsem.at[g, d - 1],
                2 * z + side_of,
            )
            copy.start()
            p_copies.append(copy)
            sends.append(copy)

    for g in range(groups):
        if g == 0:
            lo, hi = first
        else:
            lo, hi = base(pairs[g][0]), base(pairs[g][1])
        lo = lo + delta(pairs[g][0])
        hi = hi + delta(pairs[g][1])
        both = jnp.concatenate(
            [lo.reshape(n, m, chunk), hi.reshape(n, m, chunk)], axis=1
        )
        p_send[g] = both.astype(bf16).reshape(2, far, 2 * m, chunk)
        copy = remote_to(
            p_send.at[g, 1 - side_of], y_recv.at[g], y_ssem.at[g], y_rsem.at[g], partner
        )
        copy.start()
        y_copies.append(copy)
        sends.append(copy)
        if g > 0:
            spread(g - 1)
    spread(groups - 1)

    for copy in small[9:]:
        copy.wait()
    index = lax.broadcasted_iota(jnp.int32, (m, HD), 0)
    row = lax.rem(index, jnp.int32(rc))
    position = lax.div(index, jnp.int32(rc))
    for r in range(rc):
        position = position + jnp.where(row == r, len_ref[r], 0)
    angle = position.astype(f32) * freq_ref[0:1, :]
    cosine = jnp.cos(angle)
    sine = jnp.sin(angle) * freq_ref[1:2, :]

    parts = {}

    def receive(g):
        total = mid[g, place].astype(f32)
        for d in range(1, far):
            p_copies[g * (far - 1) + d - 1].wait_recv()
            total = total + p_recv[g, d - 1].astype(f32)
        parts[pairs[g][0]] = total[:m]
        parts[pairs[g][1]] = total[m:]

    def head(c, j):
        return parts[c][:, j * HD : (j + 1) * HD] * scale[:, :HD]

    def turned(block):
        swapped = jnp.concatenate([block[:, HD // 2 :], block[:, : HD // 2]], axis=1)
        return block * cosine + swapped * sine

    kc_load.wait()
    vc_load.wait()
    factor = HD ** (-0.5)
    q_rows = group * m
    cache = kc_buf.shape[2]
    q_index = lax.rem(lax.broadcasted_iota(jnp.int32, (q_rows, 1), 0), jnp.int32(m))
    q_row = lax.rem(q_index, jnp.int32(rc))
    q_step = lax.div(q_index, jnp.int32(rc))
    limit = jnp.zeros((q_rows, 1), jnp.int32)
    for r in range(rc):
        limit = limit + jnp.where(q_row == r, len_ref[r], 0)
    column = lax.broadcasted_iota(jnp.int32, (q_rows, cache), 1)
    valid = column < limit
    pad = 16
    f_col = lax.broadcasted_iota(jnp.int32, (q_rows, pad), 1)
    fresh_ok = (
        (f_col < m)
        & (lax.rem(f_col, jnp.int32(rc)) == q_row)
        & (lax.div(f_col, jnp.int32(rc)) <= q_step)
    )
    nn = (((1,), (1,)), ((), ()))
    zeros = jnp.zeros((pad - m, HD), f32)

    def attend_head(k):
        tiles = []
        for j in range(group):
            h = k * group + j
            tiles.append(turned(head(h // kv, h % kv)))
        q = jnp.concatenate(tiles, axis=0).astype(bf16)
        new_k = jnp.concatenate([turned(head(qn, k)), zeros], axis=0).astype(bf16)
        new_v = jnp.concatenate([head(qn + 1, k), zeros], axis=0).astype(bf16)
        score = jnp.zeros((q_rows, cache), f32)
        for r in range(rc):
            one = lax.dot_general(q, kc_buf[r, k], nn, preferred_element_type=f32)
            score = jnp.where(q_row == r, one, score)
        score = jnp.where(valid, score * factor, -1e30)
        fresh = lax.dot_general(q, new_k, nn, preferred_element_type=f32) * factor
        fresh = jnp.where(fresh_ok, fresh, -1e30)
        top = jnp.maximum(
            jnp.max(score, axis=1, keepdims=True), jnp.max(fresh, axis=1, keepdims=True)
        )
        e_score = jnp.exp(score - top)
        e_fresh = jnp.exp(fresh - top)
        inverse = 1.0 / (
            jnp.sum(e_score, axis=1, keepdims=True) + jnp.sum(e_fresh, axis=1, keepdims=True)
        )
        weight = (e_score * inverse).astype(bf16)
        mixed = jnp.dot(
            (e_fresh * inverse).astype(bf16), new_v, preferred_element_type=f32
        )
        for r in range(rc):
            one = jnp.dot(weight, vc_buf[r, k], preferred_element_type=f32)
            mixed = mixed + jnp.where(q_row == r, one, 0.0)
        return jnp.concatenate([mixed[j * m : (j + 1) * m] for j in range(group)], axis=1)

    receive(0)
    span = group // kv
    sides = kv // 2
    a_copies = {}

    def block_to(i, owner, slot, device):
        copy = remote_to(
            a_buf.at[i, owner],
            a_buf.at[i, owner],
            a_ssem.at[i, slot],
            a_rsem.at[i, slot],
            device,
        )
        copy.start()
        a_copies[i, slot] = copy
        sends.append(copy)

    def forward(i):
        for d in range(1, far):
            a_copies[i, d - 1].wait_recv()
            owner = 2 * lax.rem(place - d + far, far) + side_of
            block_to(i, owner, far - 1 + d, partner)

    for i in range(sides):
        for j in range(span):
            receive(1 + i * span + j)
        both = jnp.concatenate([attend_head(i), attend_head(i + sides)], axis=0)
        a_buf[i, me] = both.astype(bf16)
        for d in range(1, far):
            block_to(i, me, d - 1, 2 * lax.rem(place + d, far) + side_of)
        block_to(i, me, far - 1, partner)
        if i > 0:
            forward(i - 1)
    forward(sides - 1)

    ow_load.wait()
    size = group * HD
    u = jnp.zeros((rank, lanes), f32)
    acc = jnp.zeros((rows, ow_buf.shape[1]), f32)
    u_copies = []
    for i in range(sides):
        for slot in range(far - 1, n - 1):
            a_copies[i, slot].wait_recv()
        flat = a_buf[i].reshape(n * 2 * m, size)
        places = (i * size, (i + sides) * size)
        cols = [
            jnp.dot(back_ref[side], flat, preferred_element_type=f32).astype(bf16)
            for side in range(2)
        ]
        for at, col in zip(places, cols):
            u = u + lax.dot_general(
                od_ref[:, at : at + size], col, nn, preferred_element_type=f32
            )
        if i == sides - 1:
            u_buf[mt, me] = u
            for j, (d, e) in enumerate(others):
                copy = remote(
                    u_buf.at[mt, me], u_buf.at[mt, me], u_ssem.at[j], u_rsem.at[j], d, e
                )
                copy.start()
                u_copies.append(copy)
                sends.append(copy)
        for at, col in zip(places, cols):
            acc = acc + jnp.dot(
                col[:rows], ow_buf[at : at + size, :], preferred_element_type=f32
            )
    o_send[...] = acc
    if tp > 1:
        o_copy = remote(o_send, o_recv, o_ssem, o_rsem, 0, 1)
        o_copy.start()
        sends.append(o_copy)
    for copy in u_copies:
        copy.wait_recv()
    whole = u_buf[0]
    for t in range(1, tp):
        whole = whole + u_buf[t]
    whole = whole.reshape(n * rank, lanes).astype(bf16)
    result = lax.dot_general(whole, ou_ref[...], tn, preferred_element_type=f32)[:rows]
    result = result + x_ref[...].astype(f32)
    if tp > 1:
        o_copy.wait_recv()
        result = result + (o_send[...] + o_recv[...])
    else:
        result = result + o_send[...]
    out_ref[...] = result.astype(out_ref.dtype)
    for copy in sends:
        copy.wait_send()


def fused(n, tp, *args):
    (
        states,
        lengths,
        norm_gain,
        query_weight,
        key_weight,
        value_weight,
        out_weight,
        query_down,
        query_up,
        key_down,
        key_up,
        value_down,
        value_up,
        out_down,
        out_up,
        key_cache,
        value_cache,
    ) = args
    steps, row_total, width = states.shape
    rc = row_total // n
    rows = steps * row_total
    m = steps * rc
    rank = query_up.shape[0]
    chunk = key_weight.shape[1]
    chunks = query_weight.shape[1] // chunk + 2
    groups = chunks // 2
    lanes = -(-rows // 128) * 128
    bf16 = jnp.bfloat16
    f32 = jnp.float32

    perm = np.zeros((lanes, rows), np.float32)
    back = np.zeros((2, lanes, n * 2 * m), np.float32)
    for p in range(n):
        for s in range(steps):
            for r in range(rc):
                natural = s * row_total + p * rc + r
                perm[(p % 2 * (n // 2) + p // 2) * m + s * rc + r, natural] = 1
                for side in range(2):
                    back[side, natural, p * 2 * m + side * m + s * rc + r] = 1
    half = HD // 2
    freq = np.power(1000000.0, -(2.0 * np.arange(half)) / HD)
    table = np.zeros((8, HD), np.float32)
    table[0] = np.concatenate([freq, freq])
    table[1] = np.concatenate([-np.ones(half), np.ones(half)])

    vmem = pl.BlockSpec(memory_space=pltpu.VMEM)
    smem = pl.BlockSpec(memory_space=pltpu.SMEM)
    hbm = pl.BlockSpec(memory_space=pl.ANY)
    dma = pltpu.SemaphoreType.DMA
    kv = chunk // HD
    size = query_weight.shape[1] // kv
    out = pl.pallas_call(
        functools.partial(fused_kernel, (n, tp, steps, rc)),
        out_shape=jax.ShapeDtypeStruct((rows, width), states.dtype),
        in_specs=[smem] + [hbm] * 19,
        out_specs=vmem,
        scratch_shapes=[
            pltpu.VMEM((rows, width), bf16),
            pltpu.VMEM((width,), bf16),
            pltpu.VMEM(query_down.shape, bf16),
            pltpu.VMEM(key_down.shape, bf16),
            pltpu.VMEM(value_down.shape, bf16),
            pltpu.VMEM(query_up.shape, bf16),
            pltpu.VMEM(key_up.shape, bf16),
            pltpu.VMEM(value_up.shape, bf16),
            pltpu.VMEM(out_down.shape[::-1], bf16),
            pltpu.VMEM(out_up.shape, bf16),
            pltpu.VMEM(perm.shape, bf16),
            pltpu.VMEM(back.shape, bf16),
            pltpu.VMEM(table.shape, f32),
            pltpu.VMEM((chunks, width, chunk), bf16),
            pltpu.VMEM(out_weight.shape, bf16),
            pltpu.VMEM(key_cache.shape, bf16),
            pltpu.VMEM(value_cache.shape, bf16),
            pltpu.VMEM((n, 3 * rank + m, lanes), f32),
            pltpu.VMEM((n - 1, 3 * rank + m, lanes), f32),
            pltpu.VMEM((groups, 2, n // 2, 2 * m, chunk), bf16),
            pltpu.VMEM((groups, n // 2, 2 * m, chunk), bf16),
            pltpu.VMEM((groups, n // 2, 2 * m, chunk), bf16),
            pltpu.VMEM((groups, n // 2 - 1, 2 * m, chunk), bf16),
            pltpu.VMEM((kv // 2, n, 2 * m, size), bf16),
            pltpu.VMEM((tp, n, rank, lanes), f32),
            pltpu.VMEM((rows, width), f32),
            pltpu.VMEM((rows, width), f32),
            dma((13,)),
            dma((chunks,)),
            dma,
            dma((2,)),
            dma((n - 1,)),
            dma((n - 1,)),
            dma((groups,)),
            dma((groups,)),
            dma((groups, n // 2 - 1)),
            dma((groups, n // 2 - 1)),
            dma((kv // 2, n - 1)),
            dma((kv // 2, n - 1)),
            dma((n * tp - 1,)),
            dma((n * tp - 1,)),
            dma,
            dma,
        ],
        compiler_params=pltpu.CompilerParams(
            collective_id=0, has_side_effects=True, vmem_limit_bytes=56 * 2**20
        ),
    )(
        lengths,
        states.reshape(rows, width),
        norm_gain,
        query_down,
        key_down,
        value_down,
        query_up,
        key_up,
        value_up,
        out_down.T,
        out_up,
        jnp.asarray(perm, bf16),
        jnp.asarray(back, bf16),
        jnp.asarray(table),
        query_weight,
        key_weight,
        value_weight,
        out_weight,
        key_cache,
        value_cache,
    )
    return out.reshape(states.shape)


def fits(n, tp, states, lengths, query_weight, key_weight, query_up):
    m = states.shape[0] * lengths.shape[0]
    return (
        n > 2
        and n % 2 == 0
        and n <= 8
        and tp == 2
        and m == 8
        and states.shape[2] % 128 == 0
        and query_up.shape[0] % 16 == 0
        and key_weight.shape[1] % (2 * HD) == 0
        and query_weight.shape[1] * HD % key_weight.shape[1] ** 2 == 0
        and query_weight.shape[1] % (2 * key_weight.shape[1]) == 0
    )


def choose(n, tp, *args):
    if fits(n, tp, args[0], args[1], args[3], args[4], args[8]):
        return fused(n, tp, *args)
    return body(*args)


def solution(mesh):
    in_specs = (
        P(None, "rep", "fsdp"),
        P(("rep", "fsdp")),
        P("fsdp"),
        P("fsdp", "tp"),
        P("fsdp", "tp"),
        P("fsdp", "tp"),
        P("tp", "fsdp"),
        P("fsdp", None),
        P("fsdp", "tp"),
        P("fsdp", None),
        P("fsdp", "tp"),
        P("fsdp", None),
        P("fsdp", "tp"),
        P("tp", "fsdp"),
        P(None, "fsdp"),
        P(("rep", "fsdp"), "tp", None, None),
        P(("rep", "fsdp"), "tp", None, None),
    )
    out_specs = P(None, "rep", "fsdp")
    return jax.shard_map(functools.partial(choose, mesh.shape["fsdp"], mesh.shape["tp"]), mesh=mesh, in_specs=in_specs, out_specs=out_specs, check_vma=False)
```
